256 devices in a mesh: rep: 8 (over x_hi, y), fsdp: 32 (over z, x_lo, core).
Axes of the slice: x: 4 (x_hi: 2, x_lo: 2; x = x_hi * 2 + x_lo), y: 4, z: 8, core: 2. Of those that a mesh axis runs over, the one named last changes fastest.
Arguments:
- deltas: bfloat16 [8, 2, 1024, 8192], P('rep', None, 'fsdp'), may hold values from -2.5 to 2.5
- residual: bfloat16 [8, 2, 1024, 8192], P('rep', None, 'fsdp'), may hold values from -2.5 to 2.5
- params: float32 [2, 1024, 8192], P(None, 'fsdp'), may hold values from -6 to 6
- momentum: float32 [2, 1024, 8192], P(None, 'fsdp'), may hold values from -4 to 4
- left_sketch: bfloat16 [1024, 512], P('fsdp'), may hold values from -0.25 to 0.25
- right_hash: int32 [8192], replicated, may hold values from 0 to 1023
Outputs:
- new_params: float32 [2, 1024, 8192], P(None, 'fsdp')
- new_momentum: float32 [2, 1024, 8192], P(None, 'fsdp')
- new_residual: bfloat16 [8, 2, 1024, 8192], P('rep', None, 'fsdp')
The draws below stay inside these ranges and needn't reach their ends.
Inputs may be any that keep to these rules, and one draw needn't show every extreme that they name: right_hash % 512 is a column's bucket and right_hash // 512 (0 or 1) its sign bit.
All inputs are finite; a program needn't handle non-finite values.
Results may differ from the reference program's by a relative error of at most 0.0013.
Values sent between devices are 32-bit elements; how exact they have to be, the bound alone decides.
No kernel may reach another device: no remote copies, remote signals or barrier semaphores. Data moves between devices by JAX's collectives and lax.ppermute only.
A program may use at most 64 MiB of HBM per device.

```python
import jax
import jax.numpy as jnp
from jax import lax

N = 8192
K2 = 512
PROJ = 2
M = 1024
K1 = 512
N_REP = 8


def plant(result, stream_key, low, top_value):
    shape = result.shape
    spot = [jax.random.randint(jax.random.fold_in(stream_key, axis), (), 0, shape[axis]) for axis in range(len(shape))]
    result = result.at[tuple(spot)].set(low)
    longest = shape.index(max(shape))
    spot[longest] = (spot[longest] + 1) % shape[longest]
    return result.at[tuple(spot)].set(top_value)


def level_of(stream_key, dims, pieces, smallest, high):
    loudness = 1.0
    for dim, blocks in pieces:
        heights = jax.random.uniform(jax.random.fold_in(jax.random.fold_in(stream_key, 6), dim), (blocks,), jnp.float32, smallest / len(pieces), high / len(pieces))
        loudness = loudness * jnp.repeat(jnp.exp(heights), dims[dim] // blocks).reshape((-1,) + (1,) * (len(dims) - 1 - dim))
    return loudness


def centred(rng, shape, deviation, bound, shards=(), kind=jnp.bfloat16):
    values = jax.random.normal(rng, shape, jnp.float32) * deviation
    if len(shards) > 0:
        values = level_of(rng, shape, shards, -0.22, 0.18) * values
    return jnp.clip(values, min=-bound, max=bound).astype(kind)


def setup_inputs(seed: int = 0) -> dict:
    seeds = jax.random.split(jax.random.key(seed), 7)
    return {
        "deltas": centred(seeds[0], (N_REP, PROJ, M, N), 0.3, 2.5, ((0, 8), (2, 32))),
        "residual": centred(seeds[1], (N_REP, PROJ, M, N), 0.3, 2.5, ((0, 8), (2, 32))),
        "params": centred(seeds[2], (PROJ, M, N), 1.0, 6.0, ((1, 32),), jnp.float32),
        "momentum": centred(seeds[3], (PROJ, M, N), 0.5, 4.0, ((1, 32),), jnp.float32),
        "left_sketch": centred(seeds[4], (M, K1), K1 ** -0.5, 0.25, ((0, 32),)),
        "right_hash": plant(jax.random.randint(seeds[5], (N,), 0, 2 * K2), jax.random.fold_in(seeds[5], 1), 0, (2 * K2) - 1).astype(jnp.int32),
    }


def signed_table(right_hash, buckets):
    bucket_ids = right_hash % buckets
    column_signs = (1 - 2 * (right_hash // buckets)).astype(jnp.float32)
    columns = jnp.arange(buckets, dtype=jnp.int32)
    return jnp.where(bucket_ids[:, None] == columns[None, :], column_signs[:, None], jnp.float32(0.0))


def reference(deltas, residual, params, momentum, left_sketch, right_hash):
    highest = lax.Precision.HIGHEST
    accumulated = residual.astype(jnp.float32) + deltas.astype(jnp.float32)
    signed = signed_table(right_hash, K2)
    replica_sum = jnp.einsum('rpmn,nk->pmk', accumulated, signed, precision=highest)
    left_wide = left_sketch.astype(jnp.float32)
    compressed = jnp.einsum('mj,pmk->pjk', left_wide, replica_sum, precision=highest) / N_REP
    projected = jnp.einsum('mj,pjk->pmk', left_wide, compressed, precision=highest)
    update = jnp.einsum('pmk,nk->pmn', projected, signed, precision=highest)
    new_residual = (accumulated - update[None]).astype(jnp.bfloat16)
    new_momentum = 0.9 * momentum + update
    new_params = params - 0.7 * (update + 0.9 * new_momentum)
    return new_params, new_momentum, new_residual
```

```python
import functools

import jax
import jax.numpy as jnp
from jax import lax
from jax.experimental import pallas as pl
from jax.experimental.pallas import tpu as pltpu
from jax.sharding import Mesh, PartitionSpec as P

K2 = 512
HALF = K2 // 2
PLANE = ("xh", "y", "xl", "c")
SIZES = (("xh", 2), ("y", 4), ("z", 8), ("xl", 2), ("c", 2))
REP = ("xh", "y")
FSDP = ("z", "xl", "c")
CHUNK = 1024
NT = (((1,), (1,)), ((), ()))


def split(x):
    hi = x.astype(jnp.bfloat16)
    lo = (x - hi.astype(jnp.float32)).astype(jnp.bfloat16)
    return hi, lo


def hash_parts(h):
    sign = (1 - 2 * (h >> 9)).astype(jnp.float32)
    upper = ((h >> 8) & 1) == 1
    return h & (HALF - 1), upper, sign


def onehot(low, width):
    rows = lax.broadcasted_iota(jnp.int32, (HALF, width), 0)
    return jnp.where(rows == low, jnp.float32(1), jnp.float32(0)).astype(jnp.bfloat16)


def sketch_kernel(hash_ref, deltas_ref, residual_ref, out_ref, sum_ref):
    step = pl.program_id(0)
    width = hash_ref.shape[1]
    low, upper, sign = hash_parts(hash_ref[...])
    zero = jnp.zeros_like(sign)
    lower_sign = jnp.where(upper, zero, sign).astype(jnp.bfloat16)
    upper_sign = jnp.where(upper, sign, zero).astype(jnp.bfloat16)
    d = deltas_ref[0].reshape(-1, width)
    r = residual_ref[0].reshape(-1, width)
    wide = jnp.concatenate(
        [d * lower_sign, d * upper_sign, r * lower_sign, r * upper_sign], axis=0
    )
    part = lax.dot_general(
        onehot(low, width), wide, NT, preferred_element_type=jnp.float32
    )

    @pl.when(step == 0)
    def _():
        sum_ref[...] = part

    @pl.when(step > 0)
    def _():
        sum_ref[...] += part

    @pl.when(step == pl.num_programs(0) - 1)
    def _():
        z = sum_ref[...]
        n = z.shape[1] // 2
        out_ref[...] = (z[:, :n] + z[:, n:]).reshape(out_ref.shape)


def sketch(deltas, residual, hashes):
    _, p, m, n = deltas.shape
    block = pl.BlockSpec((1, p, m, CHUNK), lambda j: (0, 0, 0, j))
    lanes = 2 * p * m
    return pl.pallas_call(
        sketch_kernel,
        grid=(n // CHUNK,),
        in_specs=[pl.BlockSpec((1, CHUNK), lambda j: (0, j)), block, block],
        out_specs=pl.BlockSpec((32, HALF // 32, lanes), lambda j: (0, 0, 0)),
        out_shape=jax.ShapeDtypeStruct((32, HALF // 32, lanes), jnp.float32),
        scratch_shapes=[pltpu.VMEM((HALF, 2 * lanes), jnp.float32)],
        name="sketch",
    )(hashes, deltas, residual)


def left_wide(ref):
    block = ref[...].astype(jnp.bfloat16)
    return jnp.concatenate([block] * 4, axis=0)


def quarter_mask(rows):
    lane = lax.broadcasted_iota(jnp.int32, (rows, 128), 1)
    row = lax.broadcasted_iota(jnp.int32, (rows, 128), 0)
    return (lane // 32) == (row // (rows // 4))


def reduce_kernel(me_ref, recv_ref, l0, l1, l2, l3, out_ref, sum_ref):
    sum_ref[...] = jnp.sum(recv_ref[...], axis=0)
    me = me_ref[0]
    mask = quarter_mask(32)
    total = jnp.zeros(out_ref.shape, jnp.float32)
    for j, l in enumerate((l0, l1, l2, l3)):
        y = sum_ref[me ^ j]
        y = jnp.where(mask, jnp.concatenate([y] * 4, axis=0), 0.0)
        both = jnp.concatenate(split(y), axis=0)
        t = jnp.dot(both, left_wide(l), preferred_element_type=jnp.float32)
        total += t[:32] + t[32:]
    out_ref[...] = total


def reduce_columns(me, recv, lefts):
    vmem = pl.BlockSpec(memory_space=pltpu.VMEM)
    return pl.pallas_call(
        reduce_kernel,
        in_specs=[pl.BlockSpec(memory_space=pltpu.SMEM)] + [vmem] * 5,
        out_specs=vmem,
        out_shape=jax.ShapeDtypeStruct((32, lefts[0].shape[1]), jnp.float32),
        scratch_shapes=[pltpu.VMEM((4, 8, 128), jnp.float32)],
        name="reduce_columns",
    )(me, recv, *lefts)


def expand_kernel(terms, replicas, me_ref, *refs):
    parts, lefts, out_ref = refs[:terms], refs[terms : terms + 4], refs[terms + 4]
    me = me_ref[0]
    mask = quarter_mask(32)
    c = parts[0][...]
    for part in parts[1:]:
        c = c + part[...]
    both = jnp.concatenate(split(c / replicas), axis=0)
    for j, l in enumerate(lefts):
        t = lax.dot_general(
            both, left_wide(l), NT, preferred_element_type=jnp.float32
        )
        t = jnp.where(mask, t[:32] + t[32:], 0.0)
        t = t[0:8] + t[8:16] + t[16:24] + t[24:32]
        for rep in range(out_ref.shape[0]):
            out_ref[rep, me ^ j] = t


def expand_columns(me, parts, lefts, replicas):
    vmem = pl.BlockSpec(memory_space=pltpu.VMEM)
    return pl.pallas_call(
        functools.partial(expand_kernel, len(parts), replicas),
        in_specs=[pl.BlockSpec(memory_space=pltpu.SMEM)] + [vmem] * (len(parts) + 4),
        out_specs=vmem,
        out_shape=jax.ShapeDtypeStruct((8, 4, 8, 128), jnp.float32),
        name="expand_columns",
    )(me, *parts, *lefts)


def apply_kernel(
    hash_ref, p_ref, deltas_ref, residual_ref, params_ref, momentum_ref,
    new_params_ref, new_momentum_ref, new_residual_ref, left_ref,
):
    @pl.when(pl.program_id(0) == 0)
    def _():
        hi, lo = split(p_ref[...].T)
        left_ref[: hi.shape[0]] = hi
        left_ref[hi.shape[0] :] = lo

    width = hash_ref.shape[1]
    low, upper, sign = hash_parts(hash_ref[...])
    both = jnp.dot(
        left_ref[...], onehot(low, width), preferred_element_type=jnp.float32
    )
    rows = both.shape[0] // 4
    both = both[: 2 * rows] + both[2 * rows :]
    u = jnp.where(upper, both[rows:], both[:rows]) * sign
    u = u.reshape(params_ref.shape)
    acc = residual_ref[0].astype(jnp.float32) + deltas_ref[0].astype(jnp.float32)
    new_residual_ref[0] = (acc - u).astype(jnp.bfloat16)
    new_momentum = 0.9 * momentum_ref[...] + u
    new_momentum_ref[...] = new_momentum
    new_params_ref[...] = params_ref[...] - 0.7 * (u + 0.9 * new_momentum)


def apply_update(hashes, projected, deltas, residual, params, momentum):
    p, m, n = params.shape
    wide = pl.BlockSpec((p, m, CHUNK), lambda j: (0, 0, j))
    narrow = pl.BlockSpec((1, p, m, CHUNK), lambda j: (0, 0, 0, j))
    return pl.pallas_call(
        apply_kernel,
        grid=(n // CHUNK,),
        in_specs=[
            pl.BlockSpec((1, CHUNK), lambda j: (0, j)),
            pl.BlockSpec(projected.shape, lambda j: (0, 0)),
            narrow, narrow, wide, wide,
        ],
        out_specs=[wide, wide, narrow],
        out_shape=[
            jax.ShapeDtypeStruct(params.shape, jnp.float32),
            jax.ShapeDtypeStruct(momentum.shape, jnp.float32),
            jax.ShapeDtypeStruct(residual.shape, jnp.bfloat16),
        ],
        scratch_shapes=[pltpu.VMEM((4 * p * m, HALF), jnp.bfloat16)],
        name="apply_update",
    )(hashes, projected, deltas, residual, params, momentum)


def shifted(x, by):
    return lax.ppermute(x, "z", [(i, (i + by) % 8) for i in range(8)])


def sum_over_z(x):
    right = shifted(x, 1)
    left = shifted(x, -1)
    pair = x + right
    triple = pair + left
    return triple, shifted(triple, -3), shifted(pair, 2)


def per_device(deltas, residual, params, momentum, left_sketch, right_hash):
    replicas = 1
    for axis in REP:
        replicas *= lax.axis_size(axis)
    me = (lax.axis_index("xl") * 2 + lax.axis_index("c")).astype(jnp.int32).reshape(1)
    left = left_sketch.astype(jnp.float32)
    lefts = [left]
    for j in range(1, 4):
        lefts.append(lax.ppermute(left, ("xl", "c"), [(i, i ^ j) for i in range(4)]))
    hashes = right_hash.reshape(1, -1)
    sent = sketch(deltas, residual, hashes)
    recv = lax.all_to_all(sent, PLANE, 0, 0).reshape(8, 4, 8, 128)
    parts = sum_over_z(reduce_columns(me, recv, lefts))
    back = expand_columns(me, parts, lefts, replicas).reshape(32, 8, 128)
    projected = lax.all_to_all(back, PLANE, 0, 0).reshape(HALF, 128)
    return tuple(
        apply_update(hashes, projected, deltas, residual, params, momentum)
    )


def solution(mesh):
    names, sizes = zip(*SIZES)
    fine = Mesh(mesh.devices.reshape(sizes), names)
    rows = P(None, FSDP, None)
    tall = P(REP, None, FSDP, None)
    return jax.shard_map(
        per_device,
        mesh=fine,
        in_specs=(tall, tall, rows, rows, P(FSDP, None), P()),
        out_specs=(rows, rows, tall),
        check_vma=False,
    )
```

```python
import functools

import jax
import jax.numpy as jnp
import numpy as np
from jax import lax
from jax.experimental import pallas as pl
from jax.experimental.pallas import tpu as pltpu
from jax.sharding import Mesh, PartitionSpec as P

K2 = 512
HALF = K2 // 2
PAIR = 1
LEFT_FORM = 'gather'
SUM_FORM = "double"
RINGS = 8 // PAIR
SIZES = (("xh", 2), ("y", 4), ("zh", RINGS), ("z0", PAIR), ("xl", 2), ("c", 2))
REP = ("xh", "y")
FSDP = ("zh", "z0", "xl", "c")
NEAR = ("z0", "xl", "c")
GROUP = REP + NEAR
ROW_SETS = 4 * PAIR
BLOCKS = 8 * ROW_SETS
KEPT = HALF // BLOCKS
LEFT_TILES = 2
CHUNK = 2048
NT = (((1,), (1,)), ((), ()))
VMEM_BLOCK = pl.BlockSpec(memory_space=pltpu.VMEM)
HBM_BLOCK = pl.BlockSpec(memory_space=pltpu.HBM)
SMEM_BLOCK = pl.BlockSpec(memory_space=pltpu.SMEM)
PARAMS = pltpu.CompilerParams(vmem_limit_bytes=24 * 2**20)
SMALL = pltpu.CompilerParams(vmem_limit_bytes=8 * 2**20)


def in_vmem(x):
    return pltpu.with_memory_space_constraint(x, pltpu.VMEM)


def in_hbm(x):
    return pltpu.with_memory_space_constraint(x, pltpu.HBM)


def split(x):
    hi = x.astype(jnp.bfloat16)
    lo = (x - hi.astype(jnp.float32)).astype(jnp.bfloat16)
    return jnp.concatenate([hi, lo], axis=0)


def hash_parts(h):
    sign = (1 - 2 * (h >> 9)).astype(jnp.float32)
    upper = ((h >> 8) & 1) == 1
    return h & (HALF - 1), upper, sign


def onehot(low, width):
    rows = lax.broadcasted_iota(jnp.int16, (HALF, width), 0)
    return jnp.where(rows == low.astype(jnp.int16), jnp.bfloat16(1), jnp.bfloat16(0))


def sketch_kernel(
    rank_ref, hash_in, deltas_in, residual_in, left_in, out_ref,
    hash_ref, deltas_ref, residual_ref, left_ref, wide_ref, sems,
):
    pairs = (
        (hash_in, hash_ref), (left_in, left_ref),
        (deltas_in, deltas_ref), (residual_in, residual_ref),
    )
    copies = [
        pltpu.make_async_copy(there, here, sems.at[i])
        for i, (there, here) in enumerate(pairs)
    ]
    for copy in copies:
        copy.start()
    copies[0].wait()
    copies[1].wait()
    rank = rank_ref[0]
    wide_ref[...] = left_ref[...].astype(jnp.float32)
    rows = wide_ref[pl.ds(pl.multiple_of((rank >> 1) * 8, 8), 8), :]
    half = rows.shape[1] // 2
    rows = jnp.where((rank & 1) == 1, rows[:, half:], rows[:, :half])
    for i in range(LEFT_TILES):
        tile = rows[:, i * 128 : (i + 1) * 128]
        out_ref[:, (i + 1) * KEPT : (i + 2) * KEPT, :] = jnp.broadcast_to(
            tile[None], (BLOCKS,) + tile.shape
        )
    width = hash_ref.shape[1]
    low, upper, sign = hash_parts(hash_ref[...])
    zero = jnp.zeros_like(sign)
    lower_sign = jnp.where(upper, zero, sign).astype(jnp.bfloat16)
    upper_sign = jnp.where(upper, sign, zero).astype(jnp.bfloat16)
    copies[2].wait()
    copies[3].wait()
    d = deltas_ref[0].reshape(-1, width)
    r = residual_ref[0].reshape(-1, width)
    wide = jnp.concatenate(
        [d * lower_sign, d * upper_sign, r * lower_sign, r * upper_sign], axis=0
    )
    z = lax.dot_general(
        onehot(low, width), wide, NT, preferred_element_type=jnp.float32
    )
    n = z.shape[1] // 2
    out_ref[:, :KEPT, :] = (z[:, :n] + z[:, n:]).reshape(BLOCKS, KEPT, n)


def sketch(rank, hashes, deltas, residual, left):
    _, p, m, _ = deltas.shape
    arrays = (hashes, deltas, residual, left)
    return pl.pallas_call(
        sketch_kernel,
        in_specs=[SMEM_BLOCK] + [HBM_BLOCK] * 4,
        out_specs=VMEM_BLOCK,
        out_shape=pltpu.VMEM((BLOCKS, (1 + LEFT_TILES) * KEPT, 2 * p * m), jnp.float32),
        scratch_shapes=[
            *[pltpu.VMEM(x.shape, x.dtype) for x in arrays],
            pltpu.VMEM(left.shape, jnp.float32),
            pltpu.SemaphoreType.DMA((4,)),
        ],
        compiler_params=PARAMS,
        name="sketch",
    )(rank, *map(in_hbm, arrays))


def quarter_mask(rows):
    lane = lax.broadcasted_iota(jnp.int32, (rows, 128), 1)
    row = lax.broadcasted_iota(jnp.int32, (rows, 128), 0)
    return (lane // 32) == (row // (rows // 4))


def reduce_kernel(recv_ref, out_ref, left_ref):
    mask = quarter_mask(4 * KEPT)
    wide = []
    for f in range(ROW_SETS):
        rows = []
        for i in range(0, 8, 2):
            tiles = [
                recv_ref[i + j, f, (t + 1) * KEPT : (t + 2) * KEPT, :]
                for j in range(2)
                for t in range(LEFT_TILES)
            ]
            rows.append(jnp.concatenate(tiles, axis=1))
        rows = jnp.concatenate(rows, axis=0).astype(jnp.bfloat16)
        for q in range(4):
            at = (4 * f + q) * rows.shape[0]
            left_ref[at : at + rows.shape[0]] = rows
        part = jnp.sum(recv_ref[:, f, :KEPT, :], axis=0)
        wide.append(jnp.where(mask, jnp.concatenate([part] * 4, axis=0), 0.0))
    wide = split(jnp.concatenate(wide, axis=1))
    t = jnp.dot(wide, left_ref[...], preferred_element_type=jnp.float32)
    out_ref[...] = t[: 4 * KEPT] + t[4 * KEPT :]


def reduce_columns(recv, width):
    return pl.pallas_call(
        reduce_kernel,
        in_specs=[VMEM_BLOCK],
        out_specs=[VMEM_BLOCK] * 2,
        out_shape=[
            pltpu.VMEM((4 * KEPT, width), jnp.float32),
            pltpu.VMEM((128 * ROW_SETS, width), jnp.bfloat16),
        ],
        compiler_params=SMALL,
        name="reduce_columns",
    )(in_vmem(recv))


def expand_kernel(terms, replicas, *refs):
    parts, left_ref, out_ref = refs[:terms], refs[terms], refs[terms + 1]
    mask = quarter_mask(4 * KEPT)
    c = parts[0][...]
    for part in parts[1:]:
        c = c + part[...]
    wide = lax.dot_general(
        split(c / replicas), left_ref[...], NT, preferred_element_type=jnp.float32
    )
    wide = wide[: 4 * KEPT] + wide[4 * KEPT :]
    rows = []
    for f in range(ROW_SETS):
        t = jnp.where(mask, wide[:, f * 128 : (f + 1) * 128], 0.0)
        t = t[: 2 * KEPT] + t[2 * KEPT :]
        rows.append(t[:KEPT] + t[KEPT:])
    rows = jnp.concatenate(rows, axis=0)
    for rep in range(8):
        out_ref[rep * rows.shape[0] : (rep + 1) * rows.shape[0]] = rows


def expand_columns(parts, left, replicas):
    return pl.pallas_call(
        functools.partial(expand_kernel, len(parts), replicas),
        in_specs=[VMEM_BLOCK] * (len(parts) + 1),
        out_specs=VMEM_BLOCK,
        out_shape=pltpu.VMEM((HALF, 128), jnp.float32),
        compiler_params=SMALL,
        name="expand_columns",
    )(*[in_vmem(x) for x in (*parts, left)])


def apply_kernel(
    hash_ref, p_ref, deltas_in, residual_in, momentum_in, params_in,
    params_out, momentum_out, residual_out,
    deltas_ref, residual_ref, momentum_ref, params_ref,
    new_params_ref, new_momentum_ref, new_residual_ref, in_sems, out_sems,
):
    count = hash_ref.shape[1] // CHUNK

    def cut(ref, j):
        return ref.at[(slice(None),) * (len(ref.shape) - 1) + (pl.ds(j * CHUNK, CHUNK),)]

    pairs = (
        (deltas_in, deltas_ref), (residual_in, residual_ref),
        (momentum_in, momentum_ref), (params_in, params_ref),
    )
    loads = [
        [
            pltpu.make_async_copy(cut(there, j), cut(here, j), in_sems.at[i, j])
            for i, (there, here) in enumerate(pairs)
        ]
        for j in range(count)
    ]
    for group in loads:
        for copy in group:
            copy.start()
    left = split(p_ref[...].T)
    rows = left.shape[0] // 4
    stores = []
    for j in range(count):
        at = pl.ds(j * CHUNK, CHUNK)
        low, upper, sign = hash_parts(hash_ref[:, at])
        both = jnp.dot(left, onehot(low, CHUNK), preferred_element_type=jnp.float32)
        both = both[: 2 * rows] + both[2 * rows :]
        u = jnp.where(upper, both[rows:], both[:rows]) * sign
        u = u.reshape(params_ref.shape[:2] + (CHUNK,))
        for copy in loads[j]:
            copy.wait()
        d = deltas_ref[0, :, :, at].astype(jnp.float32)
        acc = residual_ref[0, :, :, at].astype(jnp.float32) + d
        new_residual_ref[0, :, :, at] = (acc - u).astype(jnp.bfloat16)
        new_momentum = 0.9 * momentum_ref[:, :, at] + u
        new_momentum_ref[:, :, at] = new_momentum
        new_params_ref[:, :, at] = params_ref[:, :, at] - 0.7 * (u + 0.9 * new_momentum)
        pairs = (
            (new_residual_ref, residual_out),
            (new_momentum_ref, momentum_out),
            (new_params_ref, params_out),
        )
        for i, (here, there) in enumerate(pairs):
            copy = pltpu.make_async_copy(cut(here, j), cut(there, j), out_sems.at[i, j])
            copy.start()
            stores.append(copy)
    for copy in stores:
        copy.wait()


def apply_update(hashes, projected, deltas, residual, momentum, params):
    wide, narrow = pltpu.VMEM(params.shape, params.dtype), pltpu.VMEM(deltas.shape, deltas.dtype)
    count = params.shape[2] // CHUNK
    return pl.pallas_call(
        apply_kernel,
        in_specs=[VMEM_BLOCK] * 2 + [HBM_BLOCK] * 4,
        out_specs=[HBM_BLOCK] * 3,
        out_shape=[
            jax.ShapeDtypeStruct(params.shape, jnp.float32),
            jax.ShapeDtypeStruct(momentum.shape, jnp.float32),
            jax.ShapeDtypeStruct(residual.shape, jnp.bfloat16),
        ],
        scratch_shapes=[
            narrow, narrow, wide, wide, wide, wide, narrow,
            pltpu.SemaphoreType.DMA((4, count)),
            pltpu.SemaphoreType.DMA((3, count)),
        ],
        compiler_params=PARAMS,
        name="apply_update",
    )(
        in_vmem(hashes), in_vmem(projected),
        *[in_hbm(x) for x in (deltas, residual, momentum, params)],
    )


def sum_over_rings(x):
    swap = lambda v, pairs: lax.ppermute(v, "zh", list(enumerate(pairs)))
    if RINGS == 8:
        x = x + swap(x, [1, 0, 3, 2, 5, 4, 7, 6])
        x = x + swap(x, [2, 3, 0, 1, 6, 7, 4, 5])
        return x, swap(x, [6, 7, 4, 5, 2, 3, 0, 1])
    x = x + swap(x, [1, 0, 3, 2])
    return x, swap(x, [3, 2, 1, 0])


AXES = tuple(name for name, _ in SIZES)
FLIP = True


def plane_groups():
    ids = np.arange(256).reshape([size for _, size in SIZES])
    if FLIP:
        ids = np.roll(ids, (1, 2, 1), (0, 1, 5))
    ids = np.moveaxis(ids, 2, 0).reshape(RINGS, -1)
    return ids.tolist()


def exchange(x):
    return lax.all_to_all(x, AXES, 0, 0, axis_index_groups=plane_groups())


def per_device(deltas, residual, params, momentum, left_sketch, right_hash):
    replicas = 1
    for axis in REP:
        replicas *= lax.axis_size(axis)
    rank = ((lax.axis_index("xh") + 1) % 2) * 4 + (lax.axis_index("y") + 2) % 4
    rank = rank.astype(jnp.int32).reshape(1)
    hashes = right_hash.reshape(1, -1)
    recv = exchange(sketch(rank, hashes, deltas, residual, left_sketch))
    recv = recv.reshape(8, ROW_SETS, (1 + LEFT_TILES) * KEPT, 128)
    reduced, left = reduce_columns(recv, left_sketch.shape[1])
    parts = sum_over_rings(reduced)
    back = expand_columns(parts, left, replicas).reshape(BLOCKS, KEPT, 128)
    projected = exchange(back).reshape(HALF, 128)
    return tuple(apply_update(hashes, projected, deltas, residual, momentum, params))


def solution(mesh):
    names, sizes = zip(*SIZES)
    fine = Mesh(mesh.devices.reshape(sizes), names)
    rows = P(None, FSDP, None)
    tall = P(REP, None, FSDP, None)
    return jax.shard_map(
        per_device,
        mesh=fine,
        in_specs=(tall, tall, rows, rows, P(FSDP, None), P()),
        out_specs=(rows, rows, tall),
        check_vma=False,
    )
```

```python
import functools

import jax
import jax.numpy as jnp
import numpy as np
from jax import lax
from jax.experimental import pallas as pl
from jax.experimental.pallas import tpu as pltpu
from jax.sharding import Mesh, PartitionSpec as P

K2 = 512
HALF = K2 // 2
PAIR = 1
LEFT_FORM = 'gather'
SUM_FORM = "double"
RINGS = 8 // PAIR
SIZES = (("xh", 2), ("y", 4), ("zh", RINGS), ("z0", PAIR), ("xl", 2), ("c", 2))
REP = ("xh", "y")
FSDP = ("zh", "z0", "xl", "c")
NEAR = ("z0", "xl", "c")
GROUP = REP + NEAR
ROW_SETS = 4 * PAIR
BLOCKS = 8 * ROW_SETS
KEPT = HALF // BLOCKS
LEFT_TILES = 2
CHUNK = 2048
FETCHED = 4096
NT = (((1,), (1,)), ((), ()))
VMEM_BLOCK = pl.BlockSpec(memory_space=pltpu.VMEM)
HBM_BLOCK = pl.BlockSpec(memory_space=pltpu.HBM)
SMEM_BLOCK = pl.BlockSpec(memory_space=pltpu.SMEM)
PARAMS = pltpu.CompilerParams(vmem_limit_bytes=24 * 2**20)
SMALL = pltpu.CompilerParams(vmem_limit_bytes=8 * 2**20)


def in_vmem(x):
    return pltpu.with_memory_space_constraint(x, pltpu.VMEM)


def in_hbm(x):
    return pltpu.with_memory_space_constraint(x, pltpu.HBM)


def split(x):
    hi = x.astype(jnp.bfloat16)
    lo = (x - hi.astype(jnp.float32)).astype(jnp.bfloat16)
    return jnp.concatenate([hi, lo], axis=0)


def hash_parts(h):
    sign = (1 - 2 * (h >> 9)).astype(jnp.float32)
    upper = ((h >> 8) & 1) == 1
    return h & (HALF - 1), upper, sign


def onehot(low, width):
    rows = lax.broadcasted_iota(jnp.int16, (HALF, width), 0)
    return jnp.where(rows == low.astype(jnp.int16), jnp.bfloat16(1), jnp.bfloat16(0))


def sketch_kernel(
    rank_ref, hash_in, deltas_in, residual_in, left_in, out_ref,
    hash_ref, deltas_ref, residual_ref, left_ref, wide_ref, sems,
):
    pairs = (
        (hash_in, hash_ref), (left_in, left_ref),
        (deltas_in, deltas_ref), (residual_in, residual_ref),
    )
    copies = [
        pltpu.make_async_copy(there, here, sems.at[i])
        for i, (there, here) in enumerate(pairs)
    ]
    for copy in copies:
        copy.start()
    copies[0].wait()
    copies[1].wait()
    rank = rank_ref[0]
    wide_ref[...] = left_ref[...].astype(jnp.float32)
    rows = wide_ref[pl.ds(pl.multiple_of((rank >> 1) * 8, 8), 8), :]
    half = rows.shape[1] // 2
    rows = jnp.where((rank & 1) == 1, rows[:, half:], rows[:, :half])
    for i in range(LEFT_TILES):
        tile = rows[:, i * 128 : (i + 1) * 128]
        out_ref[:, (i + 1) * KEPT : (i + 2) * KEPT, :] = jnp.broadcast_to(
            tile[None], (BLOCKS,) + tile.shape
        )
    width = hash_ref.shape[1]
    low, upper, sign = hash_parts(hash_ref[...])
    zero = jnp.zeros_like(sign)
    lower_sign = jnp.where(upper, zero, sign).astype(jnp.bfloat16)
    upper_sign = jnp.where(upper, sign, zero).astype(jnp.bfloat16)
    copies[2].wait()
    copies[3].wait()
    d = deltas_ref[0].reshape(-1, width)
    r = residual_ref[0].reshape(-1, width)
    wide = jnp.concatenate(
        [d * lower_sign, d * upper_sign, r * lower_sign, r * upper_sign], axis=0
    )
    z = lax.dot_general(
        onehot(low, width), wide, NT, preferred_element_type=jnp.float32
    )
    n = z.shape[1] // 2
    out_ref[:, :KEPT, :] = (z[:, :n] + z[:, n:]).reshape(BLOCKS, KEPT, n)


def sketch(rank, hashes, deltas, residual, left):
    _, p, m, _ = deltas.shape
    arrays = (hashes, deltas, residual, left)
    return pl.pallas_call(
        sketch_kernel,
        in_specs=[SMEM_BLOCK] + [HBM_BLOCK] * 4,
        out_specs=VMEM_BLOCK,
        out_shape=pltpu.VMEM((BLOCKS, (1 + LEFT_TILES) * KEPT, 2 * p * m), jnp.float32),
        scratch_shapes=[
            *[pltpu.VMEM(x.shape, x.dtype) for x in arrays],
            pltpu.VMEM(left.shape, jnp.float32),
            pltpu.SemaphoreType.DMA((4,)),
        ],
        compiler_params=PARAMS,
        name="sketch",
    )(rank, *map(in_hbm, arrays))


def quarter_mask(rows):
    lane = lax.broadcasted_iota(jnp.int32, (rows, 128), 1)
    row = lax.broadcasted_iota(jnp.int32, (rows, 128), 0)
    return (lane // 32) == (row // (rows // 4))


def reduce_kernel(recv_ref, out_ref, left_ref):
    mask = quarter_mask(4 * KEPT)
    wide = []
    for f in range(ROW_SETS):
        rows = []
        for i in range(0, 8, 2):
            tiles = [
                recv_ref[i + j, f, (t + 1) * KEPT : (t + 2) * KEPT, :]
                for j in range(2)
                for t in range(LEFT_TILES)
            ]
            rows.append(jnp.concatenate(tiles, axis=1))
        rows = jnp.concatenate(rows, axis=0).astype(jnp.bfloat16)
        for q in range(4):
            at = (4 * f + q) * rows.shape[0]
            left_ref[at : at + rows.shape[0]] = rows
        part = jnp.sum(recv_ref[:, f, :KEPT, :], axis=0)
        wide.append(jnp.where(mask, jnp.concatenate([part] * 4, axis=0), 0.0))
    wide = split(jnp.concatenate(wide, axis=1))
    t = jnp.dot(wide, left_ref[...], preferred_element_type=jnp.float32)
    out_ref[...] = t[: 4 * KEPT] + t[4 * KEPT :]


def reduce_columns(recv, width):
    return pl.pallas_call(
        reduce_kernel,
        in_specs=[VMEM_BLOCK],
        out_specs=[VMEM_BLOCK] * 2,
        out_shape=[
            pltpu.VMEM((4 * KEPT, width), jnp.float32),
            pltpu.VMEM((128 * ROW_SETS, width), jnp.bfloat16),
        ],
        compiler_params=SMALL,
        name="reduce_columns",
    )(in_vmem(recv))


def expand_kernel(terms, replicas, *refs):
    parts, left_ref, out_ref = refs[:terms], refs[terms], refs[-1]
    mask = quarter_mask(4 * KEPT)
    c = parts[0][...]
    for part in parts[1:]:
        c = c + part[...]
    wide = lax.dot_general(
        split(c / replicas), left_ref[...], NT, preferred_element_type=jnp.float32
    )
    wide = wide[: 4 * KEPT] + wide[4 * KEPT :]
    rows = []
    for f in range(ROW_SETS):
        t = jnp.where(mask, wide[:, f * 128 : (f + 1) * 128], 0.0)
        t = t[: 2 * KEPT] + t[2 * KEPT :]
        rows.append(t[:KEPT] + t[KEPT:])
    rows = jnp.concatenate(rows, axis=0)
    for rep in range(8):
        out_ref[rep * rows.shape[0] : (rep + 1) * rows.shape[0]] = rows


def expand_columns(parts, left, token, replicas):
    return pl.pallas_call(
        functools.partial(expand_kernel, len(parts), replicas),
        in_specs=[VMEM_BLOCK] * (len(parts) + 2),
        out_specs=VMEM_BLOCK,
        out_shape=pltpu.VMEM((HALF, 128), jnp.float32),
        compiler_params=SMALL,
        name="expand_columns",
    )(*[in_vmem(x) for x in (*parts, left, token)])


def columns(ref, at):
    return ref.at[(slice(None),) * (len(ref.shape) - 1) + (at,)]


def fetch_kernel(after_ref, *refs):
    count = (len(refs) - 2) // 2
    done_ref, sems = refs[count], refs[-1]
    copies = []
    for i, (there, here) in enumerate(zip(refs[:count], refs[count + 1 : -1])):
        there = columns(there, pl.ds(0, here.shape[-1]))
        copies.append(pltpu.make_async_copy(there, here, sems.at[i]))
        copies[-1].start()
    done_ref[...] = after_ref[:8, :128]
    for copy in copies:
        copy.wait()


def fetch(after, arrays):
    return pl.pallas_call(
        fetch_kernel,
        in_specs=[VMEM_BLOCK] + [HBM_BLOCK] * len(arrays),
        out_specs=[VMEM_BLOCK] * (len(arrays) + 1),
        out_shape=[
            pltpu.VMEM((8, 128), jnp.float32),
            *[pltpu.VMEM(x.shape[:-1] + (FETCHED,), x.dtype) for x in arrays],
        ],
        scratch_shapes=[pltpu.SemaphoreType.DMA((len(arrays),))],
        compiler_params=SMALL,
        cost_estimate=pl.CostEstimate(
            flops=0, bytes_accessed=6 * 2**20, transcendentals=0
        ),
        name="fetch",
    )(in_vmem(after), *map(in_hbm, arrays))


def apply_kernel(
    hash_ref, p_ref, *refs
):
    early, inputs, outputs, late, results = (refs[i : i + 4] for i in (0, 4, 8, 11, 15))
    outputs, results = outputs[:3], results[:3]
    in_sems, out_sems = refs[18:]
    count = hash_ref.shape[1] // CHUNK
    ready = FETCHED // CHUNK
    loads = []
    for j in range(ready, count):
        group = []
        for i, (there, here) in enumerate(zip(inputs, late)):
            there = columns(there, pl.ds(j * CHUNK, CHUNK))
            here = columns(here, pl.ds(j * CHUNK - FETCHED, CHUNK))
            group.append(pltpu.make_async_copy(there, here, in_sems.at[i, j - ready]))
            group[-1].start()
        loads.append(group)
    left = split(p_ref[...].T)
    rows = left.shape[0] // 4
    stores = []
    order = [j + k for j in range(ready) for k in (0, ready)]
    for j in order:
        at = pl.ds(j * CHUNK, CHUNK)
        low, upper, sign = hash_parts(hash_ref[:, at])
        both = jnp.dot(left, onehot(low, CHUNK), preferred_element_type=jnp.float32)
        both = both[: 2 * rows] + both[2 * rows :]
        u = jnp.where(upper, both[rows:], both[:rows]) * sign
        u = u.reshape(early[3].shape[:2] + (CHUNK,))
        if j >= ready:
            for copy in loads[j - ready]:
                copy.wait()
        source = early if j < ready else late
        there = pl.ds(j * CHUNK - (0 if j < ready else FETCHED), CHUNK)
        d, r, m, p = (ref[(slice(None),) * (len(ref.shape) - 1) + (there,)] for ref in source)
        acc = r[0].astype(jnp.float32) + d[0].astype(jnp.float32)
        new_residual = (acc - u).astype(jnp.bfloat16)
        new_momentum = 0.9 * m + u
        new_params = p - 0.7 * (u + 0.9 * new_momentum)
        results[2][0, :, :, at] = new_residual
        results[1][:, :, at] = new_momentum
        results[0][:, :, at] = new_params
        for i in (2, 1, 0):
            copy = pltpu.make_async_copy(
                columns(results[i], at), columns(outputs[i], at), out_sems.at[i, j]
            )
            copy.start()
            stores.append(copy)
    for copy in stores:
        copy.wait()


def apply_update(hashes, projected, early, arrays):
    deltas, _, momentum, params = arrays
    count = params.shape[2] // CHUNK
    ready = FETCHED // CHUNK
    late = [
        pltpu.VMEM(x.shape[:-1] + (x.shape[-1] - FETCHED,), x.dtype) for x in arrays
    ]
    results = [params, momentum, deltas]
    return pl.pallas_call(
        apply_kernel,
        in_specs=[VMEM_BLOCK] * 6 + [HBM_BLOCK] * 4,
        out_specs=[HBM_BLOCK] * 3,
        out_shape=[jax.ShapeDtypeStruct(x.shape, x.dtype) for x in results],
        scratch_shapes=[
            *late,
            *[pltpu.VMEM(x.shape, x.dtype) for x in results],
            pltpu.SemaphoreType.DMA((4, count - ready)),
            pltpu.SemaphoreType.DMA((3, count)),
        ],
        compiler_params=PARAMS,
        name="apply_update",
    )(in_vmem(hashes), in_vmem(projected), *map(in_vmem, early), *map(in_hbm, arrays))


def sum_over_rings(x):
    swap = lambda v, pairs: lax.ppermute(v, "zh", list(enumerate(pairs)))
    far = swap(x, [3, 2, 1, 0, 7, 6, 5, 4])
    x = x + swap(x, [1, 0, 3, 2, 5, 4, 7, 6]) + swap(x, [2, 3, 0, 1, 6, 7, 4, 5]) + far
    return x, (x, swap(x, [6, 7, 4, 5, 2, 3, 0, 1]))


AXES = tuple(name for name, _ in SIZES)
FLIP = True


def plane_groups():
    ids = np.arange(256).reshape([size for _, size in SIZES])
    if FLIP:
        ids = np.roll(ids, (1, 2, 1), (0, 1, 5))
    ids = np.moveaxis(ids, 2, 0).reshape(RINGS, -1)
    return ids.tolist()


def exchange(x):
    return lax.all_to_all(x, AXES, 0, 0, axis_index_groups=plane_groups())


def per_device(deltas, residual, params, momentum, left_sketch, right_hash):
    replicas = 1
    for axis in REP:
        replicas *= lax.axis_size(axis)
    rank = ((lax.axis_index("xh") + 1) % 2) * 4 + (lax.axis_index("y") + 2) % 4
    rank = rank.astype(jnp.int32).reshape(1)
    hashes = right_hash.reshape(1, -1)
    recv = exchange(sketch(rank, hashes, deltas, residual, left_sketch))
    recv = recv.reshape(8, ROW_SETS, (1 + LEFT_TILES) * KEPT, 128)
    reduced, left = reduce_columns(recv, left_sketch.shape[1])
    arrays = (deltas, residual, momentum, params)
    middle, parts = sum_over_rings(reduced)
    token, *early = fetch(middle, arrays)
    back = expand_columns(parts, left, token, replicas).reshape(BLOCKS, KEPT, 128)
    projected = exchange(back).reshape(HALF, 128)
    return tuple(apply_update(hashes, projected, early, arrays))


def solution(mesh):
    names, sizes = zip(*SIZES)
    fine = Mesh(mesh.devices.reshape(sizes), names)
    rows = P(None, FSDP, None)
    tall = P(REP, None, FSDP, None)
    return jax.shard_map(
        per_device,
        mesh=fine,
        in_specs=(tall, tall, rows, rows, P(FSDP, None), P()),
        out_specs=(rows, rows, tall),
        check_vma=False,
    )
```

```python
import functools

import jax
import jax.numpy as jnp
import numpy as np
from jax import lax
from jax.experimental import pallas as pl
from jax.experimental.pallas import tpu as pltpu
from jax.sharding import Mesh, PartitionSpec as P

K2 = 512
HALF = K2 // 2
PAIR = 1
LEFT_FORM = 'gather'
SUM_FORM = "double"
RINGS = 8 // PAIR
SIZES = (("xh", 2), ("y", 4), ("zh", RINGS), ("z0", PAIR), ("xl", 2), ("c", 2))
REP = ("xh", "y")
FSDP = ("zh", "z0", "xl", "c")
NEAR = ("z0", "xl", "c")
GROUP = REP + NEAR
ROW_SETS = 4 * PAIR
BLOCKS = 8 * ROW_SETS
KEPT = HALF // BLOCKS
LEFT_TILES = 2
CHUNK = 2048
FETCHED = 4096
NT = (((1,), (1,)), ((), ()))
VMEM_BLOCK = pl.BlockSpec(memory_space=pltpu.VMEM)
HBM_BLOCK = pl.BlockSpec(memory_space=pltpu.HBM)
SMEM_BLOCK = pl.BlockSpec(memory_space=pltpu.SMEM)
PARAMS = pltpu.CompilerParams(vmem_limit_bytes=24 * 2**20)
SMALL = pltpu.CompilerParams(vmem_limit_bytes=8 * 2**20)


def in_vmem(x):
    return pltpu.with_memory_space_constraint(x, pltpu.VMEM)


def in_hbm(x):
    return pltpu.with_memory_space_constraint(x, pltpu.HBM)


def split(x):
    hi = x.astype(jnp.bfloat16)
    lo = (x - hi.astype(jnp.float32)).astype(jnp.bfloat16)
    return jnp.concatenate([hi, lo], axis=0)


def hash_parts(h):
    sign = (1 - 2 * (h >> 9)).astype(jnp.float32)
    upper = ((h >> 8) & 1) == 1
    return h & (HALF - 1), upper, sign


def onehot(low, width):
    rows = lax.broadcasted_iota(jnp.int16, (HALF, width), 0)
    return jnp.where(rows == low.astype(jnp.int16), jnp.bfloat16(1), jnp.bfloat16(0))


def sketch_kernel(
    rank_ref, hash_in, deltas_in, residual_in, left_in, out_ref,
    hash_ref, deltas_ref, residual_ref, left_ref, wide_ref, sems,
):
    pairs = (
        (hash_in, hash_ref), (left_in, left_ref),
        (deltas_in, deltas_ref), (residual_in, residual_ref),
    )
    copies = [
        pltpu.make_async_copy(there, here, sems.at[i])
        for i, (there, here) in enumerate(pairs)
    ]
    for copy in copies:
        copy.start()
    copies[0].wait()
    copies[1].wait()
    rank = rank_ref[0]
    wide_ref[...] = left_ref[...].astype(jnp.float32)
    rows = wide_ref[pl.ds(pl.multiple_of((rank >> 1) * 8, 8), 8), :]
    half = rows.shape[1] // 2
    rows = jnp.where((rank & 1) == 1, rows[:, half:], rows[:, :half])
    for i in range(LEFT_TILES):
        tile = rows[:, i * 128 : (i + 1) * 128]
        out_ref[:, (i + 1) * KEPT : (i + 2) * KEPT, :] = jnp.broadcast_to(
            tile[None], (BLOCKS,) + tile.shape
        )
    width = hash_ref.shape[1]
    low, upper, sign = hash_parts(hash_ref[...])
    zero = jnp.zeros_like(sign)
    lower_sign = jnp.where(upper, zero, sign).astype(jnp.bfloat16)
    upper_sign = jnp.where(upper, sign, zero).astype(jnp.bfloat16)
    copies[2].wait()
    copies[3].wait()
    d = deltas_ref[0].reshape(-1, width)
    r = residual_ref[0].reshape(-1, width)
    wide = jnp.concatenate(
        [d * lower_sign, d * upper_sign, r * lower_sign, r * upper_sign], axis=0
    )
    z = lax.dot_general(
        onehot(low, width), wide, NT, preferred_element_type=jnp.float32
    )
    n = z.shape[1] // 2
    out_ref[:, :KEPT, :] = (z[:, :n] + z[:, n:]).reshape(BLOCKS, KEPT, n)


def sketch(rank, hashes, deltas, residual, left):
    _, p, m, _ = deltas.shape
    arrays = (hashes, deltas, residual, left)
    return pl.pallas_call(
        sketch_kernel,
        in_specs=[SMEM_BLOCK] + [HBM_BLOCK] * 4,
        out_specs=VMEM_BLOCK,
        out_shape=pltpu.VMEM((BLOCKS, (1 + LEFT_TILES) * KEPT, 2 * p * m), jnp.float32),
        scratch_shapes=[
            *[pltpu.VMEM(x.shape, x.dtype) for x in arrays],
            pltpu.VMEM(left.shape, jnp.float32),
            pltpu.SemaphoreType.DMA((4,)),
        ],
        compiler_params=PARAMS,
        name="sketch",
    )(rank, *map(in_hbm, arrays))


def quarter_mask(rows):
    lane = lax.broadcasted_iota(jnp.int32, (rows, 128), 1)
    row = lax.broadcasted_iota(jnp.int32, (rows, 128), 0)
    return (lane // 32) == (row // (rows // 4))


def reduce_kernel(recv_ref, out_ref, left_ref):
    mask = quarter_mask(4 * KEPT)
    wide = []
    for f in range(ROW_SETS):
        rows = []
        for i in range(0, 8, 2):
            tiles = [
                recv_ref[f, i + j, (t + 1) * KEPT : (t + 2) * KEPT, :]
                for j in range(2)
                for t in range(LEFT_TILES)
            ]
            rows.append(jnp.concatenate(tiles, axis=1))
        rows = jnp.concatenate(rows, axis=0).astype(jnp.bfloat16)
        for q in range(4):
            at = (4 * f + q) * rows.shape[0]
            left_ref[at : at + rows.shape[0]] = rows
        part = jnp.sum(recv_ref[f, :, :KEPT, :], axis=0)
        wide.append(jnp.where(mask, jnp.concatenate([part] * 4, axis=0), 0.0))
    wide = split(jnp.concatenate(wide, axis=1))
    t = jnp.dot(wide, left_ref[...], preferred_element_type=jnp.float32)
    out_ref[...] = t[: 4 * KEPT] + t[4 * KEPT :]


def reduce_columns(recv, width):
    return pl.pallas_call(
        reduce_kernel,
        in_specs=[VMEM_BLOCK],
        out_specs=[VMEM_BLOCK] * 2,
        out_shape=[
            pltpu.VMEM((4 * KEPT, width), jnp.float32),
            pltpu.VMEM((128 * ROW_SETS, width), jnp.bfloat16),
        ],
        compiler_params=SMALL,
        name="reduce_columns",
    )(in_vmem(recv))


def expand_kernel(terms, replicas, *refs):
    parts, left_ref, out_ref = refs[:terms], refs[terms], refs[-1]
    mask = quarter_mask(4 * KEPT)
    c = parts[0][...]
    for part in parts[1:]:
        c = c + part[...]
    wide = lax.dot_general(
        split(c / replicas), left_ref[...], NT, preferred_element_type=jnp.float32
    )
    wide = wide[: 4 * KEPT] + wide[4 * KEPT :]
    for f in range(ROW_SETS):
        t = jnp.where(mask, wide[:, f * 128 : (f + 1) * 128], 0.0)
        t = t[: 2 * KEPT] + t[2 * KEPT :]
        rows = t[:KEPT] + t[KEPT:]
        for rep in range(8):
            at = (8 * f + rep) * KEPT
            out_ref[at : at + KEPT] = rows


def expand_columns(parts, left, token, replicas):
    return pl.pallas_call(
        functools.partial(expand_kernel, len(parts), replicas),
        in_specs=[VMEM_BLOCK] * (len(parts) + 2),
        out_specs=VMEM_BLOCK,
        out_shape=pltpu.VMEM((HALF, 128), jnp.float32),
        compiler_params=SMALL,
        name="expand_columns",
    )(*[in_vmem(x) for x in (*parts, left, token)])


def columns(ref, at):
    return ref.at[(slice(None),) * (len(ref.shape) - 1) + (at,)]


def fetch_kernel(after_ref, *refs):
    count = (len(refs) - 2) // 2
    done_ref, sems = refs[count], refs[-1]
    copies = []
    for i, (there, here) in enumerate(zip(refs[:count], refs[count + 1 : -1])):
        there = columns(there, pl.ds(0, here.shape[-1]))
        copies.append(pltpu.make_async_copy(there, here, sems.at[i]))
        copies[-1].start()
    done_ref[...] = after_ref[:8, :128]
    for copy in copies:
        copy.wait()


def fetch(after, arrays):
    return pl.pallas_call(
        fetch_kernel,
        in_specs=[VMEM_BLOCK] + [HBM_BLOCK] * len(arrays),
        out_specs=[VMEM_BLOCK] * (len(arrays) + 1),
        out_shape=[
            pltpu.VMEM((8, 128), jnp.float32),
            *[pltpu.VMEM(x.shape[:-1] + (FETCHED,), x.dtype) for x in arrays],
        ],
        scratch_shapes=[pltpu.SemaphoreType.DMA((len(arrays),))],
        compiler_params=SMALL,
        cost_estimate=pl.CostEstimate(
            flops=0, bytes_accessed=6 * 2**20, transcendentals=0
        ),
        name="fetch",
    )(in_vmem(after), *map(in_hbm, arrays))


def apply_kernel(
    hash_ref, p_ref, *refs
):
    early, inputs, outputs, late, results = (refs[i : i + 4] for i in (0, 4, 8, 11, 15))
    outputs, results = outputs[:3], results[:3]
    in_sems, out_sems = refs[18:]
    count = hash_ref.shape[1] // CHUNK
    ready = FETCHED // CHUNK
    loads = []
    for j in range(ready, count):
        group = []
        for i, (there, here) in enumerate(zip(inputs, late)):
            there = columns(there, pl.ds(j * CHUNK, CHUNK))
            here = columns(here, pl.ds(j * CHUNK - FETCHED, CHUNK))
            group.append(pltpu.make_async_copy(there, here, in_sems.at[i, j - ready]))
            group[-1].start()
        loads.append(group)
    left = split(p_ref[...].T)
    rows = left.shape[0] // 4
    stores = []
    order = [j + k for j in range(ready) for k in (0, ready)]
    for j in order:
        at = pl.ds(j * CHUNK, CHUNK)
        low, upper, sign = hash_parts(hash_ref[:, at])
        both = jnp.dot(left, onehot(low, CHUNK), preferred_element_type=jnp.float32)
        both = both[: 2 * rows] + both[2 * rows :]
        u = jnp.where(upper, both[rows:], both[:rows]) * sign
        u = u.reshape(early[3].shape[:2] + (CHUNK,))
        if j >= ready:
            for copy in loads[j - ready]:
                copy.wait()
        source = early if j < ready else late
        there = pl.ds(j * CHUNK - (0 if j < ready else FETCHED), CHUNK)
        d, r, m, p = (ref[(slice(None),) * (len(ref.shape) - 1) + (there,)] for ref in source)
        acc = r[0].astype(jnp.float32) + d[0].astype(jnp.float32)
        new_residual = (acc - u).astype(jnp.bfloat16)
        new_momentum = 0.9 * m + u
        new_params = p - 0.7 * (u + 0.9 * new_momentum)
        results[2][0, :, :, at] = new_residual
        results[1][:, :, at] = new_momentum
        results[0][:, :, at] = new_params
        for i in (2, 1, 0):
            copy = pltpu.make_async_copy(
                columns(results[i], at), columns(outputs[i], at), out_sems.at[i, j]
            )
            copy.start()
            stores.append(copy)
    for copy in stores:
        copy.wait()


def apply_update(hashes, projected, early, arrays):
    deltas, _, momentum, params = arrays
    count = params.shape[2] // CHUNK
    ready = FETCHED // CHUNK
    late = [
        pltpu.VMEM(x.shape[:-1] + (x.shape[-1] - FETCHED,), x.dtype) for x in arrays
    ]
    results = [params, momentum, deltas]
    return pl.pallas_call(
        apply_kernel,
        in_specs=[VMEM_BLOCK] * 6 + [HBM_BLOCK] * 4,
        out_specs=[HBM_BLOCK] * 3,
        out_shape=[jax.ShapeDtypeStruct(x.shape, x.dtype) for x in results],
        scratch_shapes=[
            *late,
            *[pltpu.VMEM(x.shape, x.dtype) for x in results],
            pltpu.SemaphoreType.DMA((4, count - ready)),
            pltpu.SemaphoreType.DMA((3, count)),
        ],
        compiler_params=PARAMS,
        name="apply_update",
    )(in_vmem(hashes), in_vmem(projected), *map(in_vmem, early), *map(in_hbm, arrays))


def sum_over_rings(x):
    swap = lambda v, pairs: lax.ppermute(v, "zh", list(enumerate(pairs)))
    far = swap(x, [3, 2, 1, 0, 7, 6, 5, 4])
    x = x + swap(x, [1, 0, 3, 2, 5, 4, 7, 6]) + swap(x, [2, 3, 0, 1, 6, 7, 4, 5]) + far
    return x, (x, swap(x, [6, 7, 4, 5, 2, 3, 0, 1]))


AXES = tuple(name for name, _ in SIZES)
FLIP = True


def plane_groups():
    ids = np.arange(256).reshape([size for _, size in SIZES])
    if FLIP:
        ids = np.roll(ids, (1, 2, 1), (0, 1, 5))
    ids = ids.transpose(2, 3, 4, 5, 0, 1).reshape(RINGS, -1)
    return ids.tolist()


def exchange(x):
    return lax.all_to_all(x, AXES, 0, 0, axis_index_groups=plane_groups())


def per_device(deltas, residual, params, momentum, left_sketch, right_hash):
    replicas = 1
    for axis in REP:
        replicas *= lax.axis_size(axis)
    rank = ((lax.axis_index("xh") + 1) % 2) * 4 + (lax.axis_index("y") + 2) % 4
    rank = rank.astype(jnp.int32).reshape(1)
    hashes = right_hash.reshape(1, -1)
    recv = exchange(sketch(rank, hashes, deltas, residual, left_sketch))
    recv = recv.reshape(ROW_SETS, 8, (1 + LEFT_TILES) * KEPT, 128)
    reduced, left = reduce_columns(recv, left_sketch.shape[1])
    arrays = (deltas, residual, momentum, params)
    middle, parts = sum_over_rings(reduced)
    token, *early = fetch(middle, arrays)
    back = expand_columns(parts, left, token, replicas).reshape(BLOCKS, KEPT, 128)
    projected = exchange(back).reshape(HALF, 128)
    return tuple(apply_update(hashes, projected, early, arrays))


def solution(mesh):
    names, sizes = zip(*SIZES)
    fine = Mesh(mesh.devices.reshape(sizes), names)
    rows = P(None, FSDP, None)
    tall = P(REP, None, FSDP, None)
    return jax.shard_map(
        per_device,
        mesh=fine,
        in_specs=(tall, tall, rows, rows, P(FSDP, None), P()),
        out_specs=(rows, rows, tall),
        check_vma=False,
    )
```
